512 devices in a mesh: inst: 4 (over x), cell: 128 (over y, z, core).
Axes of the slice: x: 4, y: 8, z: 8, core: 2. Of those that a mesh axis runs over, the one named last changes fastest.
Arguments:
- adjoint_init: float32 [8, 384, 8, 320], P('inst', 'cell'), may hold values from -6 to 6
- source_term: float32 [8, 384, 8, 320], P('inst', 'cell'), may hold values from -6 to 6
- jacobian: bfloat16 [8, 384, 3, 320, 320], P('inst', 'cell')
- volume: float32 [384, 320], P('cell'), may hold values from 0.5 to 2
- pseudo_step: float32 [384, 320], P('cell'), may hold values from 0.2 to 0.6
- neighbor_slots: int32 [384, 3], P('cell'), may hold values from 0 to 6, as said below
- halo_blocks: int32 [512], P('cell'), may hold values from 0 to 2, as said below
- padded_rows: int32 [128], P('cell'), may hold values from 0 to 1
Outputs:
- adjoint: float32 [8, 384, 8, 320], P('inst', 'cell')
- residual: float32 [8, 384, 8, 320], P('inst', 'cell')
The draws below stay inside these ranges and needn't reach their ends.
Inputs may be any that keep to these rules, and one draw needn't show every extreme that they name: `neighbor_slots`: slot 0 of block row r is its own block, 2 + (r mod 3); slot 1 is below 2; slot 2 is 5 or more. `halo_blocks`: each device's 2 * 2 entries are its local block rows, the first 2 for the previous device, the others for the next; every entry is below 3 minus that device's padded rows.
All inputs are finite; a program needn't handle non-finite values.
Results may differ from the reference program's by a relative error of at most 0.0003.
Values sent between devices are 32-bit elements; how exact they have to be, the bound alone decides.
No kernel may reach another device: no remote copies, remote signals or barrier semaphores. Data moves between devices by JAX's collectives and lax.ppermute only.
A program may use at most 64 MiB of HBM per device.

```python
import math
import jax
import jax.numpy as jnp
from jax import lax

NT = 8
BS = 320
K = 3
HL = 2
PADMAX = 1
RB = 3
NOBJ = 8
ITERS = 16
BLOCKS = 384


def shared_pads(key):
    ncell = BLOCKS // RB
    pad_key = jax.random.fold_in(key, 101)
    counts = jax.random.randint(pad_key, (ncell,), 0, PADMAX + 1)
    counts = counts.at[0].set(PADMAX)
    counts = counts.at[1].set(0)
    return counts.astype(jnp.int32)


def draw_padded_rows(key, part):
    return shared_pads(key)


def draw_halo_blocks(key, part):
    ncell = BLOCKS // RB
    counts = shared_pads(key)
    key = jax.random.fold_in(key, 2)
    livecount = (RB - counts)[:, None]
    entries = jax.random.randint(key, (ncell, 2 * HL), 0, livecount)
    entries = entries.at[1, 0].set(0)
    entries = entries.at[1, 2 * HL - 1].set(RB - 1)
    return entries.reshape(-1).astype(jnp.int32)


def draw_neighbor_slots(key, part):
    key = jax.random.fold_in(key, 3)
    first_key, second_key = jax.random.split(key)
    rows = jnp.arange(BLOCKS, dtype=jnp.int32)
    own_slot = HL + jnp.remainder(rows, RB)
    prev_slot = jax.random.randint(first_key, (BLOCKS,), 0, HL)
    next_slot = HL + RB + jax.random.randint(second_key, (BLOCKS,), 0, HL)
    return jnp.stack([own_slot, prev_slot, next_slot], axis=1).astype(jnp.int32)


def draw_jacobian(key, part):
    key = jax.random.fold_in(key, 4)
    shape = (NT, BLOCKS, K, BS, BS)
    noise = jax.random.normal(key, shape, jnp.float32)
    noise = noise * (0.3 / BS ** 0.5)
    eye = (jnp.arange(BS)[:, None] == jnp.arange(BS)[None, :]).astype(jnp.float32)
    first = (jnp.arange(K) == 0).astype(jnp.float32)[:, None, None]
    blocks = noise + (first * eye)[None, None]
    return blocks.astype(jnp.bfloat16)


def shard_levels(key, dims, shards, smallest, largest):
    def one(position, shards_of):
        steps = jax.random.uniform(jax.random.fold_in(jax.random.fold_in(key, 6), position), (shards_of,), jnp.float32, smallest / len(shards), largest / len(shards))
        return jnp.repeat(jnp.exp(steps), dims[position] // shards_of).reshape((-1,) + (1,) * (len(dims) - position - 1))

    loudness = one(*shards[0])
    for cut in shards[1:]:
        loudness = loudness * one(*cut)
    return loudness


def scatter_about(stream_key, extent, deviation, reach, cuts=(), held_as=jnp.bfloat16):
    loudness = shard_levels(stream_key, extent, cuts, -0.22, 0.18) if cuts else 1.0
    array = jax.random.normal(stream_key, extent, jnp.float32) * deviation * loudness
    return jnp.minimum(jnp.maximum(array, -reach), reach).astype(held_as)


def setup_inputs(seed: int = 0) -> dict:
    splits = jax.random.split(jax.random.key(seed), 9)
    adjoint_init = scatter_about(splits[0], (NT, BLOCKS, NOBJ, BS), 1.0, 6.0, ((0, 4), (1, 128)), jnp.float32)
    source_term = scatter_about(splits[1], (NT, BLOCKS, NOBJ, BS), 1.0, 6.0, ((0, 4), (1, 128)), jnp.float32)
    jacobian = draw_jacobian(jax.random.fold_in(splits[8], 71), 0)
    volume = jnp.clip(jnp.exp(math.log(2.0) - 1.3862944 * jax.random.uniform(splits[3], (BLOCKS, BS), jnp.float32) ** shard_levels(splits[3], (BLOCKS, BS), ((0, 128),), -0.2, 0.2)), 0.5, 2.0)
    pseudo_step = jnp.clip(jnp.exp(math.log(0.6) - 1.0986123 * jax.random.uniform(splits[4], (BLOCKS, BS), jnp.float32) ** shard_levels(splits[4], (BLOCKS, BS), ((0, 128),), -0.2, 0.2)), 0.2, 0.6)
    neighbor_slots = draw_neighbor_slots(jax.random.fold_in(splits[8], 71), 0)
    halo_blocks = draw_halo_blocks(jax.random.fold_in(splits[8], 71), 0)
    padded_rows = draw_padded_rows(jax.random.fold_in(splits[8], 71), 0)
    return {"adjoint_init": adjoint_init, "source_term": source_term, "jacobian": jacobian, "volume": volume, "pseudo_step": pseudo_step, "neighbor_slots": neighbor_slots, "halo_blocks": halo_blocks, "padded_rows": padded_rows}


spectral_scale = 0.15


def time_matrix():
    idx = jnp.arange(NT, dtype=jnp.int32)
    diff = idx[:, None] - idx[None, :]
    parity = jnp.where(jnp.remainder(diff, 2) == 0, 1.0, -1.0).astype(jnp.float32)
    angle = jnp.float32(math.pi) * diff.astype(jnp.float32) / NT
    sine = jnp.where(diff == 0, jnp.float32(1.0), jnp.sin(angle))
    return jnp.where(diff == 0, jnp.float32(0.0), 0.5 * parity * jnp.cos(angle) / sine).astype(jnp.float32)


def reference(adjoint_init, source_term, jacobian, volume, pseudo_step, neighbor_slots, halo_blocks, padded_rows):
    ncell = BLOCKS // RB
    rows = jnp.arange(BLOCKS, dtype=jnp.int32)
    device = rows // RB
    before = jnp.remainder(device - 1, ncell).astype(jnp.int32)
    after = jnp.remainder(device + 1, ncell).astype(jnp.int32)
    lists = halo_blocks.reshape(ncell, 2 * HL)
    codes = neighbor_slots
    own_block = device[:, None] * RB + codes - HL
    pick_prev = jnp.take_along_axis(lists[before], HL + jnp.clip(codes, 0, HL - 1), axis=1)
    pick_next = jnp.take_along_axis(lists[after], jnp.clip(codes - HL - RB, 0, HL - 1), axis=1)
    from_prev = before[:, None] * RB + pick_prev
    from_next = after[:, None] * RB + pick_next
    column = jnp.where(codes < HL, from_prev, jnp.where(codes < HL + RB, own_block, from_next)).astype(jnp.int32)
    live = (jnp.remainder(rows, RB) < RB - padded_rows[device]).astype(jnp.float32)[None, :, None, None]
    weights = time_matrix()
    scale = (spectral_scale * volume)[None, :, None, :]
    step_size = pseudo_step[None, :, None, :]

    def per_instance(pair):
        plane, blocks = pair
        gathered = plane[column]
        return jnp.einsum('rkop,rkpq->roq', gathered, blocks.astype(jnp.float32), precision=lax.Precision.HIGHEST)

    adjoint = adjoint_init
    residual = jnp.zeros_like(adjoint_init)
    for sweep in range(ITERS):
        flux = lax.map(per_instance, (adjoint, jacobian))
        coupled = jnp.einsum('ji,jroq->iroq', weights, adjoint, precision=lax.Precision.HIGHEST)
        residual = live * (source_term - flux - scale * coupled)
        adjoint = adjoint + step_size * residual
    return adjoint, residual
```

```python
import functools
import math

import jax
import jax.numpy as jnp
import numpy as np
from jax import lax
from jax.experimental import pallas as pl
from jax.experimental.pallas import tpu as pltpu
from jax.sharding import PartitionSpec as P

NT = 8
ITERS = 16
SCALE = 0.15
REACH = 2
INST = 2
NEAR_PICK, FAR_PICK, LIVE, NEAR_SEND, FAR_SEND, WEIGHT, TABLE = 0, 3, 6, 9, 13, 17, 40
VMEM = pl.BlockSpec(memory_space=pltpu.VMEM)
HBM = pl.BlockSpec(memory_space=pltpu.HBM)
SMEM = pl.BlockSpec(memory_space=pltpu.SMEM)


def time_matrix():
    out = np.zeros((NT, NT))
    for j in range(NT):
        for i in range(NT):
            if i != j and (j - i) % NT != NT // 2:
                angle = math.pi * (j - i) / NT
                out[j, i] = 0.5 * (-1.0) ** (j - i) * math.cos(angle) / math.sin(angle)
    return out.astype(np.float32)


def split_rows(block):
    high = block.astype(jnp.bfloat16).astype(jnp.float32)
    return jnp.concatenate([high, block - high], axis=0).astype(jnp.bfloat16)


def product(block, matrix):
    rows = block.shape[0]
    out = jnp.dot(split_rows(block), matrix, preferred_element_type=jnp.float32)
    return out[:rows] + out[rows:]


def chosen(mask_ref, row, yes, no):
    return jnp.where(mask_ref[pl.ds(row, 1), :] > 0.0, yes, no)


def listed(tables_ref, first, entry, blocks_ref, t):
    row = first + 2 * entry
    middle = chosen(tables_ref, row, blocks_ref[t, 1], blocks_ref[t, 0])
    return chosen(tables_ref, row + 1, blocks_ref[t, 2], middle)


def tables_kernel(place_ref, slots_ref, lists_ref, pad_ref, weights_ref, tables_ref):
    width = tables_ref.shape[1]
    side = place_ref[0]
    rows = slots_ref.shape[0]

    def put(row, flag):
        tables_ref[pl.ds(row, 1), :] = jnp.full((1, width), jnp.where(flag, 1.0, 0.0), jnp.float32)

    for r in range(rows):
        put(NEAR_PICK + r, slots_ref[r, REACH - side] == 1 + (REACH + rows) * (1 - side))
        put(FAR_PICK + r, slots_ref[r, 1 + side] == 1 + (REACH + rows) * side)
        put(LIVE + r, r < rows - pad_ref[0])
    for e in range(REACH):
        for v in (1, 2):
            put(NEAR_SEND + 2 * e + v - 1, lists_ref[REACH - REACH * side + e] == v)
            put(FAR_SEND + 2 * e + v - 1, lists_ref[REACH * side + e] == v)
    inst = INST
    for j in range(NT):
        for i in range(inst):
            tables_ref[pl.ds(WEIGHT + inst * j + i, 1), :] = jnp.full(
                (1, width), weights_ref[j, place_ref[1] * inst + i], jnp.float32
            )


def send_copies(block_ref, peers_ref, sems, t):
    return [
        pltpu.make_async_copy(block_ref.at[t], peers_ref.at[p, t], sems.at[t, p])
        for p in range(peers_ref.shape[0])
    ]


def begin_kernel(place_ref, lists_ref, adjoint_ref, far_ref, peers_ref, sems):
    inst = adjoint_ref.shape[0]
    copies = [c for t in range(inst) for c in send_copies(adjoint_ref, peers_ref, sems, t)]
    for copy in copies:
        copy.start()
    for t in range(inst):
        for e in range(REACH):
            far_ref[t, e] = adjoint_ref[t, lists_ref[REACH * place_ref[0] + e]]
    for copy in copies:
        copy.wait()


def pack_kernel(place_ref, jacobian_ref, near_ref, sem):
    copy = pltpu.make_async_copy(jacobian_ref.at[:, :, REACH - place_ref[0]], near_ref, sem)
    copy.start()
    copy.wait()


def own_kernel(tables_ref, adjoint_ref, jacobian_ref, source_ref, out_ref, near_ref):
    inst, rows = adjoint_ref.shape[:2]
    for t in range(inst):
        for e in range(REACH):
            near_ref[t, e] = listed(tables_ref, NEAR_SEND, e, adjoint_ref, t)
        for r in range(rows):
            out_ref[t, r] = source_ref[t, r] - product(adjoint_ref[t, r], jacobian_ref[t, r, 0])


def picked(tables_ref, first, blocks_ref, t, r):
    return chosen(tables_ref, first + r, blocks_ref[t, 1], blocks_ref[t, 0])


def far_kernel(tables_ref, far_ref, jacobian_ref, partial_ref, out_ref):
    inst, rows = partial_ref.shape[:2]
    k = 1 + lax.rem(lax.axis_index("cell"), 2)
    for t in range(inst):
        for r in range(rows):
            flux = product(picked(tables_ref, FAR_PICK, far_ref, t, r), jacobian_ref[t, r, k])
            out_ref[t, r] = partial_ref[t, r] - flux


def update_kernel(
    last, tables_ref, near_ref, peers_ref, jacobian_ref, partial_ref, adjoint_ref, volume_ref,
    step_ref, adjoint_out, *outs
):
    inst, rows = partial_ref.shape[:2]
    copies = []
    for t in range(inst):
        for r in range(rows):
            flux = product(picked(tables_ref, NEAR_PICK, near_ref, t, r), jacobian_ref[t, r])
            coupled = None
            for p in range(peers_ref.shape[0]):
                for j in range(inst):
                    row = WEIGHT + inst * (p * inst + j) + t
                    term = tables_ref[pl.ds(row, 1), :] * peers_ref[p, j, r]
                    coupled = term if coupled is None else coupled + term
            scale = SCALE * volume_ref[pl.ds(r, 1), :]
            live = tables_ref[pl.ds(LIVE + r, 1), :]
            residual = live * (partial_ref[t, r] - flux - scale * coupled)
            adjoint_out[t, r] = adjoint_ref[t, r] + step_ref[pl.ds(r, 1), :] * residual
            if last:
                outs[0][t, r] = residual
        if not last:
            far_out, peers_out, sems = outs
            started = send_copies(adjoint_out, peers_out, sems, t)
            for copy in started:
                copy.start()
            copies += started
            for e in range(REACH):
                far_out[t, e] = listed(tables_ref, FAR_SEND, e, adjoint_out, t)
    for copy in copies:
        copy.wait()


def call(kernel, ins, outs, *args, scratch=(), cost=None):
    spaces = {"s": SMEM, "v": VMEM, "a": HBM}
    return pl.pallas_call(
        kernel,
        in_specs=[spaces[c] for c in ins],
        out_specs=[spaces[c] for c, _ in outs],
        out_shape=[jax.ShapeDtypeStruct(*o) for _, o in outs],
        scratch_shapes=list(scratch),
        compiler_params=pltpu.CompilerParams(vmem_limit_bytes=4 << 20),
        cost_estimate=cost and pl.CostEstimate(flops=0, bytes_accessed=cost, transcendentals=0),
    )(*args)


def on_device(adjoint, source, jacobian, volume, step, slots, lists, pads):
    inst, rows, objectives, width = adjoint.shape
    peers = lax.axis_size("inst")
    cells = lax.axis_size("cell")
    near_pairs = [(i, i ^ 1) for i in range(cells)]
    far_pairs = [(i, (i + 1 if i % 2 else i - 1) % cells) for i in range(cells)]
    side = lax.rem(lax.axis_index("cell"), 2).astype(jnp.int32)
    place = jnp.stack([side, lax.axis_index("inst").astype(jnp.int32)])
    f32 = jnp.float32
    block = (adjoint.shape, f32)
    halo = ((inst, REACH, objectives, width), f32)
    gathered = ((peers,) + adjoint.shape, f32)
    packed = ((inst, rows, width, width), jacobian.dtype)
    sends = [pltpu.SemaphoreType.DMA((inst, peers))]
    far, spread = call(
        begin_kernel, "ssv", (("v", halo), ("a", gathered)), place, lists, adjoint, scratch=sends
    )
    tables = call(
        tables_kernel, "sssss", (("v", ((TABLE, width), f32)),), place, slots, lists, pads,
        jnp.asarray(time_matrix()),
    )[0]
    near_j = call(
        pack_kernel, "sa", (("v", packed),), place, jacobian, scratch=[pltpu.SemaphoreType.DMA]
    )[0]
    for sweep in range(ITERS):
        last = sweep == ITERS - 1
        spread = lax.all_to_all(spread, "inst", 0, 0)
        far = lax.ppermute(far, "cell", far_pairs)
        partial, near = call(
            own_kernel, "vvvv", (("v", block), ("v", halo)), tables, adjoint, jacobian, source
        )
        near = lax.ppermute(near, "cell", near_pairs)
        partial = call(far_kernel, "vvvv", (("v", block),), tables, far, jacobian, partial)[0]
        outs = (("v", block),) * 2 if last else (("v", block), ("v", halo), ("a", gathered))
        result = call(
            functools.partial(update_kernel, last), "vvvvvvvv", outs,
            tables, near, spread, near_j, partial, adjoint, volume, step,
            scratch=[] if last else sends,
        )
        if last:
            return result[0], result[1]
        adjoint, far, spread = result


def solution(mesh):
    return jax.shard_map(
        on_device,
        mesh=mesh,
        in_specs=(
            P("inst", "cell", None, None),
            P("inst", "cell", None, None),
            P("inst", "cell", None, None, None),
            P("cell", None),
            P("cell", None),
            P("cell", None),
            P("cell"),
            P("cell"),
        ),
        out_specs=(P("inst", "cell", None, None), P("inst", "cell", None, None)),
        check_vma=False,
    )
```

```python
import functools
import math

import jax
import jax.numpy as jnp
import numpy as np
from jax import lax
from jax.experimental import pallas as pl
from jax.experimental.pallas import tpu as pltpu
from jax.sharding import PartitionSpec as P

NT = 8
ITERS = 16
SCALE = 0.15
REACH = 2
INST = 2
NEAR_PICK, FAR_PICK, LIVE, NEAR_SEND, FAR_SEND, SAME, CROSS, TABLE = 0, 3, 6, 9, 13, 17, 21, 32
VMEM = pl.BlockSpec(memory_space=pltpu.VMEM)
HBM = pl.BlockSpec(memory_space=pltpu.HBM)
SMEM = pl.BlockSpec(memory_space=pltpu.SMEM)


def time_matrix():
    out = np.zeros((NT, NT))
    for j in range(NT):
        for i in range(NT):
            if i != j and (j - i) % NT != NT // 2:
                angle = math.pi * (j - i) / NT
                out[j, i] = 0.5 * (-1.0) ** (j - i) * math.cos(angle) / math.sin(angle)
    return out.astype(np.float32)


def swapped(block):
    return pltpu.roll(block, block.shape[1] // 2, 1)


def product(block, matrix):
    rows, lanes = block.shape
    width = lanes // 2
    parts = []
    for half in (block[:, :width], swapped(block)[:, :width]):
        for _ in range(3):
            part = half.astype(jnp.bfloat16).astype(jnp.float32)
            parts.append(part)
            half = half - part
    stacked = jnp.concatenate(parts, axis=0).astype(jnp.bfloat16)
    out = jnp.dot(stacked, matrix, preferred_element_type=jnp.float32)
    first, second = (
        out[n : n + rows] + out[n + rows : n + 2 * rows] + out[n + 2 * rows : n + 3 * rows]
        for n in (0, 3 * rows)
    )
    lane = lax.broadcasted_iota(jnp.int32, (rows, lanes), 1)
    return jnp.where(lane < width, first, second)


def chosen(mask_ref, row, yes, no):
    return jnp.where(mask_ref[pl.ds(row, 1), :] > 0.0, yes, no)


def listed(tables_ref, first, entry, blocks_ref):
    row = first + 2 * entry
    middle = chosen(tables_ref, row, blocks_ref[1], blocks_ref[0])
    return chosen(tables_ref, row + 1, blocks_ref[2], middle)


def tables_kernel(place_ref, slots_ref, lists_ref, pad_ref, weights_ref, tables_ref):
    lanes = tables_ref.shape[1]
    side = place_ref[0]
    first = INST * place_ref[1]
    rows = slots_ref.shape[0]
    lane = lax.broadcasted_iota(jnp.int32, (1, lanes), 1)

    def put(row, left, right):
        tables_ref[pl.ds(row, 1), :] = jnp.where(lane < lanes // 2, left, right)

    def flag(row, holds):
        value = jnp.where(holds, 1.0, 0.0).astype(jnp.float32)
        put(row, value, value)

    for r in range(rows):
        flag(NEAR_PICK + r, slots_ref[r, REACH - side] == 1 + (REACH + rows) * (1 - side))
        flag(FAR_PICK + r, slots_ref[r, 1 + side] == 1 + (REACH + rows) * side)
        flag(LIVE + r, r < rows - pad_ref[0])
    for e in range(REACH):
        for v in (1, 2):
            flag(NEAR_SEND + 2 * e + v - 1, lists_ref[REACH - REACH * side + e] == v)
            flag(FAR_SEND + 2 * e + v - 1, lists_ref[REACH * side + e] == v)
    for p in range(NT // INST):
        put(SAME + p, weights_ref[2 * p, first], weights_ref[2 * p + 1, first + 1])
        put(CROSS + p, weights_ref[2 * p, first + 1], weights_ref[2 * p + 1, first])


def send_copies(block_ref, peers_ref, sems, r):
    return [
        pltpu.make_async_copy(block_ref.at[r], peers_ref.at[p, r], sems.at[r, p])
        for p in range(peers_ref.shape[0])
    ]


def begin_kernel(place_ref, lists_ref, adjoint_ref, near_ref, far_ref, peers_ref, sems):
    side = place_ref[0]
    rows = adjoint_ref.shape[0]
    copies = [c for r in range(rows) for c in send_copies(adjoint_ref, peers_ref, sems, r)]
    for copy in copies:
        copy.start()
    for e in range(REACH):
        near_ref[e] = adjoint_ref[lists_ref[REACH - REACH * side + e]]
        far_ref[e] = adjoint_ref[lists_ref[REACH * side + e]]
    for copy in copies:
        copy.wait()


def here_kernel(tables_ref, adjoint_ref, near_ref, own_j_ref, near_j_ref, source_ref, out_ref):
    other = 1 - lax.rem(lax.axis_index("cell"), 2)
    for r in range(adjoint_ref.shape[0]):
        own = product(adjoint_ref[r], own_j_ref[r])
        block = chosen(tables_ref, NEAR_PICK + r, near_ref[other, 1], near_ref[other, 0])
        out_ref[r] = source_ref[r] - (own + product(block, near_j_ref[r]))


def update_kernel(
    last, tables_ref, far_ref, far_j_ref, peers_ref, partial_ref, adjoint_ref, volume_ref,
    step_ref, *outs
):
    rows, _, lanes = adjoint_ref.shape
    width = lanes // 2
    copies = []
    for r in range(rows):
        block = chosen(tables_ref, FAR_PICK + r, far_ref[1], far_ref[0])
        flux = product(block, far_j_ref[r])
        same = cross = None
        for p in range(peers_ref.shape[0]):
            one = tables_ref[pl.ds(SAME + p, 1), :] * peers_ref[p, r]
            two = tables_ref[pl.ds(CROSS + p, 1), :] * peers_ref[p, r]
            same, cross = (one, two) if same is None else (same + one, cross + two)
        coupled = same + swapped(cross)
        scale = SCALE * volume_ref[pl.ds(r, 1), :]
        live = tables_ref[pl.ds(LIVE + r, 1), :]
        residual = live * (partial_ref[r] - flux - scale * coupled)
        new = adjoint_ref[r] + step_ref[pl.ds(r, 1), :] * residual
        if last:
            for value, out_ref in zip((new, residual), outs):
                out_ref[0, r] = value[:, :width]
                out_ref[1, r] = swapped(value)[:, :width]
            continue
        outs[0][r] = new
        started = send_copies(outs[0], outs[3], outs[4], r)
        for copy in started:
            copy.start()
        copies += started
    if not last:
        for e in range(REACH):
            outs[1][e] = listed(tables_ref, NEAR_SEND, e, outs[0])
            outs[2][e] = listed(tables_ref, FAR_SEND, e, outs[0])
    for copy in copies:
        copy.wait()


def call(kernel, ins, outs, *args, scratch=(), cost=None):
    spaces = {"s": SMEM, "v": VMEM, "a": HBM}
    return pl.pallas_call(
        kernel,
        in_specs=[spaces[c] for c in ins],
        out_specs=[spaces[c] for c, _ in outs],
        out_shape=[jax.ShapeDtypeStruct(*o) for _, o in outs],
        scratch_shapes=list(scratch),
        compiler_params=pltpu.CompilerParams(vmem_limit_bytes=4 << 20),
        cost_estimate=cost and pl.CostEstimate(flops=cost, bytes_accessed=0, transcendentals=0),
    )(*args)


def side_by_side(blocks):
    return jnp.concatenate([blocks[0], blocks[1]], axis=-1)


def on_device(adjoint, source, jacobian, volume, step, slots, lists, pads):
    shape = adjoint.shape
    _, rows, objectives, width = shape
    peers = lax.axis_size("inst")
    cells = lax.axis_size("cell")
    near_groups = [[i, i + 1] for i in range(0, cells, 2)]
    far_pairs = [(i, (i + 1 if i % 2 else i - 1) % cells) for i in range(cells)]
    side = lax.rem(lax.axis_index("cell"), 2).astype(jnp.int32)
    place = jnp.stack([side, lax.axis_index("inst").astype(jnp.int32)])
    f32 = jnp.float32
    lanes = 2 * width
    block = ((rows, objectives, lanes), f32)
    halo = ((REACH, objectives, lanes), f32)
    gathered = ((peers,) + block[0], f32)
    sends = [pltpu.SemaphoreType.DMA((rows, peers))]
    listed_out = (("v", halo), ("v", halo), ("a", gathered))
    adjoint = side_by_side(adjoint)
    near, far, spread = call(
        begin_kernel, "ssv", listed_out, place, lists, adjoint, scratch=sends
    )
    tables = call(
        tables_kernel, "sssss", (("v", ((TABLE, lanes), f32)),), place, slots, lists, pads,
        jnp.asarray(time_matrix()),
    )[0]
    source = side_by_side(source)
    volume = jnp.concatenate([volume, volume], axis=-1)
    step = jnp.concatenate([step, step], axis=-1)
    own_j, near_j, far_j = (
        side_by_side(lax.dynamic_index_in_dim(jacobian, k, axis=2, keepdims=False))
        for k in (0, REACH - side, 1 + side)
    )
    for sweep in range(ITERS):
        last = sweep == ITERS - 1
        spread = lax.all_to_all(spread, "inst", 0, 0)
        far = lax.ppermute(far, "cell", far_pairs)
        near = lax.all_gather(near, "cell", axis_index_groups=near_groups)
        partial = call(
            here_kernel, "vvvvvv", (("v", block),), tables, adjoint, near, own_j, near_j, source
        )[0]
        result = call(
            functools.partial(update_kernel, last), "vvvvvvvv",
            (("v", (shape, f32)),) * 2 if last else (("v", block),) + listed_out,
            tables, far, far_j, spread, partial, adjoint, volume, step,
            scratch=[] if last else sends,
        )
        if last:
            return result[0], result[1]
        adjoint, near, far, spread = result


def solution(mesh):
    return jax.shard_map(
        on_device,
        mesh=mesh,
        in_specs=(
            P("inst", "cell", None, None),
            P("inst", "cell", None, None),
            P("inst", "cell", None, None, None),
            P("cell", None),
            P("cell", None),
            P("cell", None),
            P("cell"),
            P("cell"),
        ),
        out_specs=(P("inst", "cell", None, None), P("inst", "cell", None, None)),
        check_vma=False,
    )
```

```python
import functools
import math

import jax
import jax.numpy as jnp
import numpy as np
from jax import lax
from jax.experimental import pallas as pl
from jax.experimental.pallas import tpu as pltpu
from jax.sharding import PartitionSpec as P

NT = 8
ITERS = 16
SCALE = 0.15
REACH = 2
INST = 2
NEAR_PICK, FAR_PICK, LIVE, NEAR_SEND, FAR_SEND, SAME, CROSS, TABLE = 0, 3, 6, 9, 13, 17, 21, 32
VMEM = pl.BlockSpec(memory_space=pltpu.VMEM)
HBM = pl.BlockSpec(memory_space=pltpu.HBM)
SMEM = pl.BlockSpec(memory_space=pltpu.SMEM)


def time_matrix():
    out = np.zeros((NT, NT))
    for j in range(NT):
        for i in range(NT):
            if i != j and (j - i) % NT != NT // 2:
                angle = math.pi * (j - i) / NT
                out[j, i] = 0.5 * (-1.0) ** (j - i) * math.cos(angle) / math.sin(angle)
    return out.astype(np.float32)


def swapped(block):
    return pltpu.roll(block, block.shape[1] // 2, 1)


def product(block, matrix):
    rows, lanes = block.shape
    width = lanes // 2
    parts = []
    for half in (block[:, :width], swapped(block)[:, :width]):
        for _ in range(3):
            part = half.astype(jnp.bfloat16).astype(jnp.float32)
            parts.append(part)
            half = half - part
    stacked = jnp.concatenate(parts, axis=0).astype(jnp.bfloat16)
    out = jnp.dot(stacked, matrix, preferred_element_type=jnp.float32)
    first, second = (
        out[n : n + rows] + out[n + rows : n + 2 * rows] + out[n + 2 * rows : n + 3 * rows]
        for n in (0, 3 * rows)
    )
    return jnp.where(lane_of((rows, lanes)) < width, first, second)


def chosen(mask_ref, row, yes, no):
    return jnp.where(mask_ref[pl.ds(row, 1), :] > 0.0, yes, no)


def listed(tables_ref, first, entry, blocks_ref):
    row = first + 2 * entry
    middle = chosen(tables_ref, row, blocks_ref[1], blocks_ref[0])
    return chosen(tables_ref, row + 1, blocks_ref[2], middle)


def tables_kernel(
    slots_ref, lists_ref, pad_ref, weights_ref, source_ref, volume_ref, step_ref,
    tables_ref, source_out, volume_out, step_out, held
):
    lanes = tables_ref.shape[1]
    side = lax.rem(lax.axis_index("cell"), 2)
    first = INST * lax.axis_index("inst")
    rows = slots_ref.shape[0]
    lane = lane_of((1, lanes))
    for r in range(rows):
        source_out[r] = side_by_side(held, source_ref[0, r], source_ref[1, r])
        for value_ref, out_ref in ((volume_ref, volume_out), (step_ref, step_out)):
            value = jnp.broadcast_to(value_ref[pl.ds(r, 1), :], source_ref.shape[2:])
            out_ref[pl.ds(r, 1), :] = side_by_side(held, value, value)[:1]

    def put(row, left, right):
        tables_ref[pl.ds(row, 1), :] = jnp.where(lane < lanes // 2, left, right)

    def flag(row, holds):
        value = jnp.where(holds, 1.0, 0.0).astype(jnp.float32)
        put(row, value, value)

    for r in range(rows):
        flag(NEAR_PICK + r, slots_ref[r, REACH - side] == 1 + (REACH + rows) * (1 - side))
        flag(FAR_PICK + r, slots_ref[r, 1 + side] == 1 + (REACH + rows) * side)
        flag(LIVE + r, r < rows - pad_ref[0])
    for e in range(REACH):
        for v in (1, 2):
            flag(NEAR_SEND + 2 * e + v - 1, lists_ref[REACH - REACH * side + e] == v)
            flag(FAR_SEND + 2 * e + v - 1, lists_ref[REACH * side + e] == v)
    for p in range(NT // INST):
        put(SAME + p, weights_ref[2 * p, first], weights_ref[2 * p + 1, first + 1])
        put(CROSS + p, weights_ref[2 * p, first + 1], weights_ref[2 * p + 1, first])


def send_copy(held, peers_ref, sems, r):
    return pltpu.make_async_copy(held.at[:, r], peers_ref.at[:, r], sems.at[r])


def lane_of(shape):
    return lax.broadcasted_iota(jnp.int32, shape, len(shape) - 1)


def side_by_side(held, left, right):
    width = held.shape[1] // 2
    held[:, :width] = right
    moved = swapped(held[...])
    held[:, :width] = left
    return jnp.where(lane_of(held.shape) < width, held[...], moved)


def begin_kernel(
    lists_ref, adjoint_ref, adjoint_out, near_ref, far_ref, peers_ref, held, copied, sems
):
    side = lax.rem(lax.axis_index("cell"), 2)
    copies = []
    for r in range(adjoint_out.shape[0]):
        new = side_by_side(held, adjoint_ref[0, r], adjoint_ref[1, r])
        adjoint_out[r] = new
        for p in range(copied.shape[0]):
            copied[p, r] = new
        copies.append(send_copy(copied, peers_ref, sems, r))
        copies[-1].start()
    for e in range(REACH):
        near_ref[e] = adjoint_out[lists_ref[REACH - REACH * side + e]]
        far_ref[e] = adjoint_out[lists_ref[REACH * side + e]]
    for copy in copies:
        copy.wait()


def pack_kernel(jacobian_ref, own_ref, near_ref, far_ref, held):
    rows = jacobian_ref.shape[1]
    side = lax.rem(lax.axis_index("cell"), 2)
    height = held.shape[0]
    for k, out_ref in ((0, own_ref), (REACH - side, near_ref), (1 + side, far_ref)):
        for r in range(rows):

            @pl.loop(0, out_ref.shape[1] // height)
            def _(n):
                some = pl.ds(pl.multiple_of(n * height, height), height)
                left, right = (
                    jacobian_ref[t, r, k, some, :].astype(jnp.float32) for t in range(INST)
                )
                out_ref[r, some, :] = side_by_side(held, left, right).astype(out_ref.dtype)


def here_kernel(tables_ref, adjoint_ref, near_ref, own_j_ref, near_j_ref, source_ref, out_ref):
    other = 1 - lax.rem(lax.axis_index("cell"), 2)
    for r in range(adjoint_ref.shape[0]):
        own = product(adjoint_ref[r], own_j_ref[r])
        block = chosen(tables_ref, NEAR_PICK + r, near_ref[other, 1], near_ref[other, 0])
        out_ref[r] = source_ref[r] - (own + product(block, near_j_ref[r]))


def update_kernel(
    last, tables_ref, far_ref, far_j_ref, peers_ref, partial_ref, adjoint_ref, volume_ref,
    step_ref, *outs
):
    rows, _, lanes = adjoint_ref.shape
    width = lanes // 2
    copies = []
    for r in range(rows):
        block = chosen(tables_ref, FAR_PICK + r, far_ref[1], far_ref[0])
        flux = product(block, far_j_ref[r])
        same = cross = None
        for p in range(peers_ref.shape[0]):
            one = tables_ref[pl.ds(SAME + p, 1), :] * peers_ref[p, r]
            two = tables_ref[pl.ds(CROSS + p, 1), :] * peers_ref[p, r]
            same, cross = (one, two) if same is None else (same + one, cross + two)
        coupled = same + swapped(cross)
        scale = SCALE * volume_ref[pl.ds(r, 1), :]
        live = tables_ref[pl.ds(LIVE + r, 1), :]
        residual = live * (partial_ref[r] - flux - scale * coupled)
        new = adjoint_ref[r] + step_ref[pl.ds(r, 1), :] * residual
        if last:
            for value, out_ref in zip((new, residual), outs):
                out_ref[0, r] = value[:, :width]
                out_ref[1, r] = swapped(value)[:, :width]
            continue
        outs[0][r] = new
        for p in range(peers_ref.shape[0]):
            outs[4][p, r] = new
        copies.append(send_copy(outs[4], outs[3], outs[5], r))
        copies[-1].start()
    if not last:
        for e in range(REACH):
            outs[1][e] = listed(tables_ref, NEAR_SEND, e, outs[0])
            outs[2][e] = listed(tables_ref, FAR_SEND, e, outs[0])
    for copy in copies:
        copy.wait()


def call(kernel, ins, outs, *args, scratch=()):
    spaces = {"s": SMEM, "v": VMEM, "a": HBM}
    return pl.pallas_call(
        kernel,
        in_specs=[spaces[c] for c in ins],
        out_specs=[spaces[c] for c, _ in outs],
        out_shape=[jax.ShapeDtypeStruct(*o) for _, o in outs],
        scratch_shapes=list(scratch),
        compiler_params=pltpu.CompilerParams(vmem_limit_bytes=4 << 20),
    )(*args)


def on_device(adjoint, source, jacobian, volume, step, slots, lists, pads):
    shape = adjoint.shape
    _, rows, objectives, width = shape
    peers = lax.axis_size("inst")
    cells = lax.axis_size("cell")
    near_groups = [[i, i + 1] for i in range(0, cells, 2)]
    far_pairs = [(i, (i + 1 if i % 2 else i - 1) % cells) for i in range(cells)]
    f32 = jnp.float32
    lanes = 2 * width
    block = ((rows, objectives, lanes), f32)
    halo = ((REACH, objectives, lanes), f32)
    gathered = ((peers,) + block[0], f32)
    sends = [pltpu.VMEM(*gathered), pltpu.SemaphoreType.DMA((rows,))]
    listed_out = (("v", block), ("v", halo), ("v", halo), ("a", gathered))
    held = pltpu.VMEM(block[0][1:], f32)
    adjoint, near, far, spread = call(
        begin_kernel, "sv", listed_out, lists, adjoint, scratch=[held] + sends
    )
    cells_out = ("v", ((rows, lanes), f32))
    tables, source, volume, step = call(
        tables_kernel, "ssssvvv", (("v", ((TABLE, lanes), f32)), ("v", block)) + (cells_out,) * 2,
        slots, lists, pads, jnp.asarray(time_matrix()), source, volume, step, scratch=[held],
    )
    own_j, near_j, far_j = call(
        pack_kernel, "v", (("v", ((rows, width, lanes), jacobian.dtype)),) * 3, jacobian,
        scratch=[pltpu.VMEM((64, lanes), f32)],
    )
    for sweep in range(ITERS):
        last = sweep == ITERS - 1
        spread = lax.all_to_all(spread, "inst", 0, 0)
        far = lax.ppermute(far, "cell", far_pairs)
        near = lax.all_gather(near, "cell", axis_index_groups=near_groups)
        partial = call(
            here_kernel, "vvvvvv", (("v", block),), tables, adjoint, near, own_j, near_j, source
        )[0]
        result = call(
            functools.partial(update_kernel, last), "vvvvvvvv",
            (("v", (shape, f32)),) * 2 if last else listed_out,
            tables, far, far_j, spread, partial, adjoint, volume, step,
            scratch=[] if last else sends,
        )
        if last:
            return result[0], result[1]
        adjoint, near, far, spread = result


def solution(mesh):
    return jax.shard_map(
        on_device,
        mesh=mesh,
        in_specs=(
            P("inst", "cell", None, None),
            P("inst", "cell", None, None),
            P("inst", "cell", None, None, None),
            P("cell", None),
            P("cell", None),
            P("cell", None),
            P("cell"),
            P("cell"),
        ),
        out_specs=(P("inst", "cell", None, None), P("inst", "cell", None, None)),
        check_vma=False,
    )
```

```python
import functools
import math

import jax
import jax.numpy as jnp
import numpy as np
from jax import lax
from jax.experimental import pallas as pl
from jax.experimental.pallas import tpu as pltpu
from jax.sharding import PartitionSpec as P

NT = 8
ITERS = 16
SCALE = 0.15
REACH = 2
INST = 2
TILE = 128
NEAR_PICK, FAR_PICK, LIVE, NEAR_SEND, FAR_SEND, SAME, CROSS, TABLE = 0, 3, 6, 9, 13, 17, 21, 32
VMEM = pl.BlockSpec(memory_space=pltpu.VMEM)
HBM = pl.BlockSpec(memory_space=pltpu.HBM)
SMEM = pl.BlockSpec(memory_space=pltpu.SMEM)


def time_matrix():
    out = np.zeros((NT, NT))
    for j in range(NT):
        for i in range(NT):
            if i != j and (j - i) % NT != NT // 2:
                angle = math.pi * (j - i) / NT
                out[j, i] = 0.5 * (-1.0) ** (j - i) * math.cos(angle) / math.sin(angle)
    return out.astype(np.float32)


def cut_of(width):
    return width - width % TILE


def lane_of(shape):
    return lax.broadcasted_iota(jnp.int32, shape, len(shape) - 1)


def in_left(shape):
    width = shape[-1] // 2
    cut, lane = cut_of(width), lane_of(shape)
    return (lane < cut) | ((lane >= 2 * cut) & (lane < cut + width))


def left_of(block):
    width = block.shape[1] // 2
    cut = cut_of(width)
    return jnp.concatenate([block[:, :cut], block[:, 2 * cut : cut + width]], axis=1)


def swapped(block):
    width = block.shape[1] // 2
    cut = cut_of(width)
    tail = pltpu.roll(block[:, 2 * cut :], width - cut, 1)
    return jnp.concatenate([block[:, cut : 2 * cut], block[:, :cut], tail], axis=1)


def tail_beside(held, left, right):
    size = left.shape[1]
    held[:, :size] = right
    moved = pltpu.roll(held[...], size, 1)
    held[:, :size] = left
    return jnp.where(lane_of(held.shape) < size, held[...], moved)


def side_by_side(held, left, right):
    cut = cut_of(left.shape[1])
    tail = tail_beside(held, left[:, cut:], right[:, cut:])
    return jnp.concatenate([left[:, :cut], right[:, :cut], tail], axis=1)


def product(block, matrix):
    rows, lanes = block.shape
    parts = []
    for half in (left_of(block), left_of(swapped(block))):
        for _ in range(3):
            part = half.astype(jnp.bfloat16).astype(jnp.float32)
            parts.append(part)
            half = half - part
    stacked = jnp.concatenate(parts, axis=0).astype(jnp.bfloat16)
    out = jnp.dot(stacked, matrix, preferred_element_type=jnp.float32)
    first, second = (
        out[n : n + rows] + out[n + rows : n + 2 * rows] + out[n + 2 * rows : n + 3 * rows]
        for n in (0, 3 * rows)
    )
    return jnp.where(in_left((rows, lanes)), first, second)


def chosen(mask_ref, row, yes, no):
    return jnp.where(mask_ref[pl.ds(row, 1), :] > 0.0, yes, no)


def listed(tables_ref, first, entry, blocks_ref):
    row = first + 2 * entry
    middle = chosen(tables_ref, row, blocks_ref[1], blocks_ref[0])
    return chosen(tables_ref, row + 1, blocks_ref[2], middle)


def tables_kernel(
    slots_ref, lists_ref, pad_ref, weights_ref, source_ref, volume_ref, step_ref,
    tables_ref, source_out, volume_out, step_out, held
):
    lanes = tables_ref.shape[1]
    side = lax.rem(lax.axis_index("cell"), 2)
    first = INST * lax.axis_index("inst")
    rows = slots_ref.shape[0]
    is_left = in_left((1, lanes))
    for r in range(rows):
        source_out[r] = side_by_side(held, source_ref[0, r], source_ref[1, r])
        for value_ref, out_ref in ((volume_ref, volume_out), (step_ref, step_out)):
            value = jnp.broadcast_to(value_ref[pl.ds(r, 1), :], source_ref.shape[2:])
            out_ref[pl.ds(r, 1), :] = side_by_side(held, value, value)[:1]

    def put(row, left, right):
        tables_ref[pl.ds(row, 1), :] = jnp.where(is_left, left, right)

    def flag(row, holds):
        value = jnp.where(holds, 1.0, 0.0).astype(jnp.float32)
        put(row, value, value)

    for r in range(rows):
        flag(NEAR_PICK + r, slots_ref[r, REACH - side] == 1 + (REACH + rows) * (1 - side))
        flag(FAR_PICK + r, slots_ref[r, 1 + side] == 1 + (REACH + rows) * side)
        flag(LIVE + r, r < rows - pad_ref[0])
    for e in range(REACH):
        for v in (1, 2):
            flag(NEAR_SEND + 2 * e + v - 1, lists_ref[REACH - REACH * side + e] == v)
            flag(FAR_SEND + 2 * e + v - 1, lists_ref[REACH * side + e] == v)
    for p in range(NT // INST):
        put(SAME + p, weights_ref[2 * p, first], weights_ref[2 * p + 1, first + 1])
        put(CROSS + p, weights_ref[2 * p, first + 1], weights_ref[2 * p + 1, first])


def send_copy(held, peers_ref, sems, r):
    return pltpu.make_async_copy(held.at[:, r], peers_ref.at[:, r], sems.at[r])


def begin_kernel(adjoint_ref, adjoint_out, peers_ref, held, copied, sems):
    copies = []
    for r in range(adjoint_out.shape[0]):
        new = side_by_side(held, adjoint_ref[0, r], adjoint_ref[1, r])
        adjoint_out[r] = new
        for p in range(copied.shape[0]):
            copied[p, r] = new
        copies.append(send_copy(copied, peers_ref, sems, r))
        copies[-1].start()
    for copy in copies:
        copy.wait()


def lists_kernel(lists_ref, adjoint_ref, near_ref, far_ref):
    side = lax.rem(lax.axis_index("cell"), 2)
    for e in range(REACH):
        near_ref[e] = adjoint_ref[lists_ref[REACH - REACH * side + e]]
        far_ref[e] = adjoint_ref[lists_ref[REACH * side + e]]


def pack_kernel(jacobian_ref, own_ref, near_ref, far_ref, held):
    rows, width = jacobian_ref.shape[1], jacobian_ref.shape[-1]
    side = lax.rem(lax.axis_index("cell"), 2)
    cut = cut_of(width)
    for k, out_ref in ((0, own_ref), (REACH - side, near_ref), (1 + side, far_ref)):
        for r in range(rows):
            for t in range(INST):
                out_ref[r, :, t * cut : (t + 1) * cut] = jacobian_ref[t, r, k, :, :cut]
            left, right = (
                jacobian_ref[t, r, k, :, cut:].astype(jnp.float32) for t in range(INST)
            )
            out_ref[r, :, 2 * cut :] = tail_beside(held, left, right).astype(out_ref.dtype)


def here_kernel(tables_ref, adjoint_ref, near_ref, own_j_ref, near_j_ref, source_ref, out_ref):
    other = 1 - lax.rem(lax.axis_index("cell"), 2)
    for r in range(adjoint_ref.shape[0]):
        own = product(adjoint_ref[r], own_j_ref[r])
        block = chosen(tables_ref, NEAR_PICK + r, near_ref[other, 1], near_ref[other, 0])
        out_ref[r] = source_ref[r] - (own + product(block, near_j_ref[r]))


def update_kernel(
    last, tables_ref, far_ref, far_j_ref, peers_ref, partial_ref, adjoint_ref, volume_ref,
    step_ref, *outs
):
    rows = adjoint_ref.shape[0]
    copies = []
    for r in range(rows):
        block = chosen(tables_ref, FAR_PICK + r, far_ref[1], far_ref[0])
        flux = product(block, far_j_ref[r])
        same = cross = None
        for p in range(peers_ref.shape[0]):
            one = tables_ref[pl.ds(SAME + p, 1), :] * peers_ref[p, r]
            two = tables_ref[pl.ds(CROSS + p, 1), :] * peers_ref[p, r]
            same, cross = (one, two) if same is None else (same + one, cross + two)
        coupled = same + swapped(cross)
        scale = SCALE * volume_ref[pl.ds(r, 1), :]
        live = tables_ref[pl.ds(LIVE + r, 1), :]
        residual = live * (partial_ref[r] - flux - scale * coupled)
        new = adjoint_ref[r] + step_ref[pl.ds(r, 1), :] * residual
        if last:
            for value, out_ref in zip((new, residual), outs):
                out_ref[0, r] = left_of(value)
                out_ref[1, r] = left_of(swapped(value))
            continue
        outs[0][r] = new
        for p in range(peers_ref.shape[0]):
            outs[4][p, r] = new
        copies.append(send_copy(outs[4], outs[3], outs[5], r))
        copies[-1].start()
    if not last:
        for e in range(REACH):
            outs[1][e] = listed(tables_ref, NEAR_SEND, e, outs[0])
            outs[2][e] = listed(tables_ref, FAR_SEND, e, outs[0])
    for copy in copies:
        copy.wait()


def call(kernel, ins, outs, *args, scratch=()):
    spaces = {"s": SMEM, "v": VMEM, "a": HBM}
    return pl.pallas_call(
        kernel,
        in_specs=[spaces[c] for c in ins],
        out_specs=[spaces[c] for c, _ in outs],
        out_shape=[jax.ShapeDtypeStruct(*o) for _, o in outs],
        scratch_shapes=list(scratch),
        compiler_params=pltpu.CompilerParams(vmem_limit_bytes=4 << 20),
    )(*args)


def on_device(adjoint, source, jacobian, volume, step, slots, lists, pads):
    shape = adjoint.shape
    _, rows, objectives, width = shape
    peers = lax.axis_size("inst")
    cells = lax.axis_size("cell")
    near_groups = [[i, i + 1] for i in range(0, cells, 2)]
    far_pairs = [(i, (i + 1 if i % 2 else i - 1) % cells) for i in range(cells)]
    f32 = jnp.float32
    lanes = 2 * width
    block = ((rows, objectives, lanes), f32)
    halo = ((REACH, objectives, lanes), f32)
    gathered = ((peers,) + block[0], f32)
    sends = [pltpu.VMEM(*gathered), pltpu.SemaphoreType.DMA((rows,))]
    listed_out = (("v", block), ("v", halo), ("v", halo), ("a", gathered))
    held = pltpu.VMEM((objectives, TILE), f32)
    adjoint, spread = call(
        begin_kernel, "v", (("v", block), ("a", gathered)), adjoint, scratch=[held] + sends
    )
    near, far = call(lists_kernel, "sv", (("v", halo),) * 2, lists, adjoint)
    cells_out = ("v", ((rows, lanes), f32))
    tables, source, volume, step = call(
        tables_kernel, "ssssvvv", (("v", ((TABLE, lanes), f32)), ("v", block)) + (cells_out,) * 2,
        slots, lists, pads, jnp.asarray(time_matrix()), source, volume, step, scratch=[held],
    )
    own_j, near_j, far_j = call(
        pack_kernel, "v", (("v", ((rows, width, lanes), jacobian.dtype)),) * 3, jacobian,
        scratch=[pltpu.VMEM((width, TILE), f32)],
    )
    for sweep in range(ITERS):
        last = sweep == ITERS - 1
        spread = lax.all_to_all(spread, "inst", 0, 0)
        far = lax.ppermute(far, "cell", far_pairs)
        near = lax.all_gather(near, "cell", axis_index_groups=near_groups)
        partial = call(
            here_kernel, "vvvvvv", (("v", block),), tables, adjoint, near, own_j, near_j, source
        )[0]
        result = call(
            functools.partial(update_kernel, last), "vvvvvvvv",
            (("v", (shape, f32)),) * 2 if last else listed_out,
            tables, far, far_j, spread, partial, adjoint, volume, step,
            scratch=[] if last else sends,
        )
        if last:
            return result[0], result[1]
        adjoint, near, far, spread = result


def solution(mesh):
    return jax.shard_map(
        on_device,
        mesh=mesh,
        in_specs=(
            P("inst", "cell", None, None),
            P("inst", "cell", None, None),
            P("inst", "cell", None, None, None),
            P("cell", None),
            P("cell", None),
            P("cell", None),
            P("cell"),
            P("cell"),
        ),
        out_specs=(P("inst", "cell", None, None), P("inst", "cell", None, None)),
        check_vma=False,
    )
```

```python
import functools
import math

import jax
import jax.numpy as jnp
import numpy as np
from jax import lax
from jax.experimental import pallas as pl
from jax.experimental.pallas import tpu as pltpu
from jax.sharding import PartitionSpec as P

NT = 8
ITERS = 16
SCALE = 0.15
REACH = 2
INST = 2
TILE = 128
NEAR_PICK, FAR_PICK, LIVE, NEAR_SEND, FAR_SEND, SAME, CROSS, TABLE = 0, 3, 6, 9, 13, 17, 21, 32
VMEM = pl.BlockSpec(memory_space=pltpu.VMEM)
HBM = pl.BlockSpec(memory_space=pltpu.HBM)
SMEM = pl.BlockSpec(memory_space=pltpu.SMEM)


def time_matrix():
    out = np.zeros((NT, NT))
    for j in range(NT):
        for i in range(NT):
            if i != j and (j - i) % NT != NT // 2:
                angle = math.pi * (j - i) / NT
                out[j, i] = 0.5 * (-1.0) ** (j - i) * math.cos(angle) / math.sin(angle)
    return out.astype(np.float32)


def cut_of(width):
    return width - width % TILE


def lane_of(shape):
    return lax.broadcasted_iota(jnp.int32, shape, len(shape) - 1)


def in_left(shape):
    width = shape[-1] // 2
    cut, lane = cut_of(width), lane_of(shape)
    return (lane < cut) | ((lane >= 2 * cut) & (lane < cut + width))


def left_of(block):
    width = block.shape[1] // 2
    cut = cut_of(width)
    return jnp.concatenate([block[:, :cut], block[:, 2 * cut : cut + width]], axis=1)


def swapped(block):
    width = block.shape[1] // 2
    cut = cut_of(width)
    tail = pltpu.roll(block[:, 2 * cut :], width - cut, 1)
    return jnp.concatenate([block[:, cut : 2 * cut], block[:, :cut], tail], axis=1)


def tail_beside(held, left, right):
    size = left.shape[1]
    held[:, :size] = right
    moved = pltpu.roll(held[...], size, 1)
    held[:, :size] = left
    return jnp.where(lane_of(held.shape) < size, held[...], moved)


def side_by_side(held, left, right):
    cut = cut_of(left.shape[1])
    tail = tail_beside(held, left[:, cut:], right[:, cut:])
    return jnp.concatenate([left[:, :cut], right[:, :cut], tail], axis=1)


def product(block, matrix):
    rows, lanes = block.shape
    parts = []
    for half in (left_of(block), left_of(swapped(block))):
        for _ in range(3):
            part = half.astype(jnp.bfloat16).astype(jnp.float32)
            parts.append(part)
            half = half - part
    stacked = jnp.concatenate(parts, axis=0).astype(jnp.bfloat16)
    out = jnp.dot(stacked, matrix, preferred_element_type=jnp.float32)
    first, second = (
        out[n : n + rows] + out[n + rows : n + 2 * rows] + out[n + 2 * rows : n + 3 * rows]
        for n in (0, 3 * rows)
    )
    return jnp.where(in_left((rows, lanes)), first, second)


def chosen(mask_ref, row, yes, no):
    return jnp.where(mask_ref[pl.ds(row, 1), :] > 0.0, yes, no)


def listed(tables_ref, first, entry, blocks_ref):
    row = first + 2 * entry
    middle = chosen(tables_ref, row, blocks_ref[1], blocks_ref[0])
    return chosen(tables_ref, row + 1, blocks_ref[2], middle)


def tables_kernel(
    slots_ref, lists_ref, pad_ref, weights_ref, source_ref, volume_ref, step_ref,
    tables_ref, source_out, volume_out, step_out, held
):
    lanes = tables_ref.shape[1]
    side = lax.rem(lax.axis_index("cell"), 2)
    first = INST * lax.axis_index("inst")
    rows = slots_ref.shape[0]
    is_left = in_left((1, lanes))
    for r in range(rows):
        source_out[r] = side_by_side(held, source_ref[0, r], source_ref[1, r])
        for value_ref, out_ref in ((volume_ref, volume_out), (step_ref, step_out)):
            value = jnp.broadcast_to(value_ref[pl.ds(r, 1), :], source_ref.shape[2:])
            out_ref[pl.ds(r, 1), :] = side_by_side(held, value, value)[:1]

    def put(row, left, right):
        tables_ref[pl.ds(row, 1), :] = jnp.where(is_left, left, right)

    def flag(row, holds):
        value = jnp.where(holds, 1.0, 0.0).astype(jnp.float32)
        put(row, value, value)

    for r in range(rows):
        flag(NEAR_PICK + r, slots_ref[r, REACH - side] == 1 + (REACH + rows) * (1 - side))
        flag(FAR_PICK + r, slots_ref[r, 1 + side] == 1 + (REACH + rows) * side)
        flag(LIVE + r, r < rows - pad_ref[0])
    for e in range(REACH):
        for v in (1, 2):
            flag(NEAR_SEND + 2 * e + v - 1, lists_ref[REACH - REACH * side + e] == v)
            flag(FAR_SEND + 2 * e + v - 1, lists_ref[REACH * side + e] == v)
    for p in range(NT // INST):
        put(SAME + p, weights_ref[2 * p, first], weights_ref[2 * p + 1, first + 1])
        put(CROSS + p, weights_ref[2 * p, first + 1], weights_ref[2 * p + 1, first])


def begin_kernel(adjoint_ref, adjoint_out, peers_ref, tail, held, sem):
    for r in range(adjoint_out.shape[0]):
        new = side_by_side(tail, adjoint_ref[0, r], adjoint_ref[1, r])
        adjoint_out[r] = new
        for p in range(held.shape[0]):
            held[p, r] = new
    copy = pltpu.make_async_copy(held, peers_ref, sem)
    copy.start()
    copy.wait()


def lists_kernel(lists_ref, adjoint_ref, near_ref, far_ref):
    side = lax.rem(lax.axis_index("cell"), 2)
    for e in range(REACH):
        near_ref[e] = adjoint_ref[lists_ref[REACH - REACH * side + e]]
        far_ref[e] = adjoint_ref[lists_ref[REACH * side + e]]


def pack_kernel(jacobian_ref, own_ref, near_ref, far_ref, held):
    rows, width = jacobian_ref.shape[1], jacobian_ref.shape[-1]
    side = lax.rem(lax.axis_index("cell"), 2)
    cut = cut_of(width)
    for k, out_ref in ((0, own_ref), (REACH - side, near_ref), (1 + side, far_ref)):
        for r in range(rows):
            for t in range(INST):
                out_ref[r, :, t * cut : (t + 1) * cut] = jacobian_ref[t, r, k, :, :cut]
            left, right = (
                jacobian_ref[t, r, k, :, cut:].astype(jnp.float32) for t in range(INST)
            )
            out_ref[r, :, 2 * cut :] = tail_beside(held, left, right).astype(out_ref.dtype)


def here_kernel(
    tables_ref, adjoint_ref, near_ref, peers_ref, own_j_ref, near_j_ref, source_ref, volume_ref,
    out_ref
):
    other = 1 - lax.rem(lax.axis_index("cell"), 2)
    for r in range(adjoint_ref.shape[0]):
        own = product(adjoint_ref[r], own_j_ref[r])
        block = chosen(tables_ref, NEAR_PICK + r, near_ref[other, 1], near_ref[other, 0])
        near = product(block, near_j_ref[r])
        same = cross = None
        for p in range(peers_ref.shape[0]):
            one = tables_ref[pl.ds(SAME + p, 1), :] * peers_ref[p, r]
            two = tables_ref[pl.ds(CROSS + p, 1), :] * peers_ref[p, r]
            same, cross = (one, two) if same is None else (same + one, cross + two)
        coupled = same + swapped(cross)
        scale = SCALE * volume_ref[pl.ds(r, 1), :]
        out_ref[r] = source_ref[r] - (own + near) - scale * coupled


def update_kernel(
    last, tables_ref, far_ref, far_j_ref, partial_ref, adjoint_ref, step_ref, *outs
):
    rows = adjoint_ref.shape[0]
    fluxes = [
        product(chosen(tables_ref, FAR_PICK + r, far_ref[1], far_ref[0]), far_j_ref[r])
        for r in range(rows)
    ]
    residuals, news = [], []
    for r, flux in enumerate(fluxes):
        live = tables_ref[pl.ds(LIVE + r, 1), :]
        residuals.append(live * (partial_ref[r] - flux))
        news.append(adjoint_ref[r] + step_ref[pl.ds(r, 1), :] * residuals[r])
    if last:
        for values, out_ref in zip((news, residuals), outs):
            for r, value in enumerate(values):
                out_ref[0, r] = left_of(value)
                out_ref[1, r] = left_of(swapped(value))
        return
    adjoint_out, near_out, far_out, peers_out, held, sem = outs
    for r, new in enumerate(news):
        for p in range(held.shape[0]):
            held[p, r] = new
    copy = pltpu.make_async_copy(held, peers_out, sem)
    copy.start()
    for r, new in enumerate(news):
        adjoint_out[r] = new
    for e in range(REACH):
        near_out[e] = listed(tables_ref, NEAR_SEND, e, news)
        far_out[e] = listed(tables_ref, FAR_SEND, e, news)
    copy.wait()


def call(kernel, ins, outs, *args, scratch=()):
    spaces = {"s": SMEM, "v": VMEM, "a": HBM}
    return pl.pallas_call(
        kernel,
        in_specs=[spaces[c] for c in ins],
        out_specs=[spaces[c] for c, _ in outs],
        out_shape=[jax.ShapeDtypeStruct(*o) for _, o in outs],
        scratch_shapes=list(scratch),
        compiler_params=pltpu.CompilerParams(vmem_limit_bytes=4 << 20),
    )(*args)


def on_device(adjoint, source, jacobian, volume, step, slots, lists, pads):
    shape = adjoint.shape
    _, rows, objectives, width = shape
    peers = lax.axis_size("inst")
    cells = lax.axis_size("cell")
    near_groups = [[i, i + 1] for i in range(0, cells, 2)]
    far_pairs = [(i, (i + 1 if i % 2 else i - 1) % cells) for i in range(cells)]
    f32 = jnp.float32
    lanes = 2 * width
    block = ((rows, objectives, lanes), f32)
    halo = ((REACH, objectives, lanes), f32)
    gathered = ((peers,) + block[0], f32)
    sends = [pltpu.VMEM(*gathered), pltpu.SemaphoreType.DMA]
    listed_out = (("v", block), ("v", halo), ("v", halo), ("a", gathered))
    held = pltpu.VMEM((objectives, TILE), f32)
    adjoint, spread = call(
        begin_kernel, "v", (("v", block), ("a", gathered)), adjoint, scratch=[held] + sends
    )
    near, far = call(lists_kernel, "sv", (("v", halo),) * 2, lists, adjoint)
    cells_out = ("v", ((rows, lanes), f32))
    tables, source, volume, step = call(
        tables_kernel, "ssssvvv", (("v", ((TABLE, lanes), f32)), ("v", block)) + (cells_out,) * 2,
        slots, lists, pads, jnp.asarray(time_matrix()), source, volume, step, scratch=[held],
    )
    own_j, near_j, far_j = call(
        pack_kernel, "v", (("v", ((rows, width, lanes), jacobian.dtype)),) * 3, jacobian,
        scratch=[pltpu.VMEM((width, TILE), f32)],
    )
    for sweep in range(ITERS):
        last = sweep == ITERS - 1
        spread = lax.all_to_all(spread, "inst", 0, 0)
        far = lax.ppermute(far, "cell", far_pairs)
        near = lax.all_gather(near, "cell", axis_index_groups=near_groups)
        partial = call(
            here_kernel, "vvvvvvvv", (("v", block),),
            tables, adjoint, near, spread, own_j, near_j, source, volume,
        )[0]
        result = call(
            functools.partial(update_kernel, last), "vvvvvv",
            (("v", (shape, f32)),) * 2 if last else listed_out,
            tables, far, far_j, partial, adjoint, step, scratch=[] if last else sends,
        )
        if last:
            return result[0], result[1]
        adjoint, near, far, spread = result


def solution(mesh):
    return jax.shard_map(
        on_device,
        mesh=mesh,
        in_specs=(
            P("inst", "cell", None, None),
            P("inst", "cell", None, None),
            P("inst", "cell", None, None, None),
            P("cell", None),
            P("cell", None),
            P("cell", None),
            P("cell"),
            P("cell"),
        ),
        out_specs=(P("inst", "cell", None, None), P("inst", "cell", None, None)),
        check_vma=False,
    )
```

```python
import functools
import math

import jax
import jax.numpy as jnp
import numpy as np
from jax import lax
from jax.experimental import pallas as pl
from jax.experimental.pallas import tpu as pltpu
from jax.sharding import PartitionSpec as P

NT = 8
ITERS = 16
SCALE = 0.15
REACH = 2
INST = 2
TILE = 128
NEAR_PICK, FAR_PICK, LIVE, NEAR_SEND, FAR_SEND, SAME, CROSS, TABLE = 0, 3, 6, 9, 13, 17, 21, 32
VMEM = pl.BlockSpec(memory_space=pltpu.VMEM)
HBM = pl.BlockSpec(memory_space=pltpu.HBM)
SMEM = pl.BlockSpec(memory_space=pltpu.SMEM)


def time_matrix():
    out = np.zeros((NT, NT))
    for j in range(NT):
        for i in range(NT):
            if i != j and (j - i) % NT != NT // 2:
                angle = math.pi * (j - i) / NT
                out[j, i] = 0.5 * (-1.0) ** (j - i) * math.cos(angle) / math.sin(angle)
    return out.astype(np.float32)


def cut_of(width):
    return width - width % TILE


def lane_of(shape):
    return lax.broadcasted_iota(jnp.int32, shape, len(shape) - 1)


def in_left(shape):
    width = shape[-1] // 2
    cut, lane = cut_of(width), lane_of(shape)
    return (lane < cut) | ((lane >= 2 * cut) & (lane < cut + width))


def left_of(block):
    width = block.shape[1] // 2
    cut = cut_of(width)
    return jnp.concatenate([block[:, :cut], block[:, 2 * cut : cut + width]], axis=1)


def swapped(block):
    width = block.shape[1] // 2
    cut = cut_of(width)
    tail = pltpu.roll(block[:, 2 * cut :], width - cut, 1)
    return jnp.concatenate([block[:, cut : 2 * cut], block[:, :cut], tail], axis=1)


def tail_beside(held, left, right):
    size = left.shape[1]
    held[:, :size] = right
    moved = pltpu.roll(held[...], size, 1)
    held[:, :size] = left
    return jnp.where(lane_of(held.shape) < size, held[...], moved)


def side_by_side(held, left, right):
    cut = cut_of(left.shape[1])
    tail = tail_beside(held, left[:, cut:], right[:, cut:])
    return jnp.concatenate([left[:, :cut], right[:, :cut], tail], axis=1)


def product(block, matrix):
    rows, lanes = block.shape
    parts = []
    for half in (left_of(block), left_of(swapped(block))):
        for _ in range(3):
            part = half.astype(jnp.bfloat16).astype(jnp.float32)
            parts.append(part)
            half = half - part
    stacked = jnp.concatenate(parts, axis=0).astype(jnp.bfloat16)
    out = jnp.dot(stacked, matrix, preferred_element_type=jnp.float32)
    first, second = (
        out[n : n + rows] + out[n + rows : n + 2 * rows] + out[n + 2 * rows : n + 3 * rows]
        for n in (0, 3 * rows)
    )
    return jnp.where(in_left((rows, lanes)), first, second)


def chosen(mask_ref, row, yes, no):
    return jnp.where(mask_ref[pl.ds(row, 1), :] > 0.0, yes, no)


def listed(tables_ref, first, entry, blocks_ref):
    row = first + 2 * entry
    middle = chosen(tables_ref, row, blocks_ref[1], blocks_ref[0])
    return chosen(tables_ref, row + 1, blocks_ref[2], middle)


def tables_kernel(
    slots_ref, lists_ref, pad_ref, weights_ref, source_ref, volume_ref, step_ref,
    tables_ref, source_out, volume_out, step_out, held
):
    lanes = tables_ref.shape[1]
    side = lax.rem(lax.axis_index("cell"), 2)
    first = INST * lax.axis_index("inst")
    rows = slots_ref.shape[0]
    is_left = in_left((1, lanes))
    for r in range(rows):
        source_out[r] = side_by_side(held, source_ref[0, r], source_ref[1, r])
        for value_ref, out_ref in ((volume_ref, volume_out), (step_ref, step_out)):
            value = jnp.broadcast_to(value_ref[pl.ds(r, 1), :], source_ref.shape[2:])
            out_ref[pl.ds(r, 1), :] = side_by_side(held, value, value)[:1]

    def put(row, left, right):
        tables_ref[pl.ds(row, 1), :] = jnp.where(is_left, left, right)

    def flag(row, holds):
        value = jnp.where(holds, 1.0, 0.0).astype(jnp.float32)
        put(row, value, value)

    for r in range(rows):
        flag(NEAR_PICK + r, slots_ref[r, REACH - side] == 1 + (REACH + rows) * (1 - side))
        flag(FAR_PICK + r, slots_ref[r, 1 + side] == 1 + (REACH + rows) * side)
        flag(LIVE + r, r < rows - pad_ref[0])
    for e in range(REACH):
        for v in (1, 2):
            flag(NEAR_SEND + 2 * e + v - 1, lists_ref[REACH - REACH * side + e] == v)
            flag(FAR_SEND + 2 * e + v - 1, lists_ref[REACH * side + e] == v)
    for p in range(NT // INST):
        put(SAME + p, weights_ref[2 * p, first], weights_ref[2 * p + 1, first + 1])
        put(CROSS + p, weights_ref[2 * p, first + 1], weights_ref[2 * p + 1, first])


def send_copy(held, peers_ref, sems, r):
    return pltpu.make_async_copy(held.at[:, r], peers_ref.at[:, r], sems.at[r])


def begin_kernel(
    lists_ref, adjoint_ref, adjoint_out, near_ref, far_ref, peers_ref, held, copied, sems
):
    side = lax.rem(lax.axis_index("cell"), 2)
    copies = []
    for r in range(adjoint_out.shape[0]):
        new = side_by_side(held, adjoint_ref[0, r], adjoint_ref[1, r])
        adjoint_out[r] = new
        for p in range(copied.shape[0]):
            copied[p, r] = new
        copies.append(send_copy(copied, peers_ref, sems, r))
        copies[-1].start()
    for e in range(REACH):
        near_ref[e] = adjoint_out[lists_ref[REACH - REACH * side + e]]
        far_ref[e] = adjoint_out[lists_ref[REACH * side + e]]
    for copy in copies:
        copy.wait()


def pack_kernel(jacobian_ref, own_ref, near_ref, far_ref, held):
    rows, width = jacobian_ref.shape[1], jacobian_ref.shape[-1]
    side = lax.rem(lax.axis_index("cell"), 2)
    cut = cut_of(width)
    for k, out_ref in ((0, own_ref), (REACH - side, near_ref), (1 + side, far_ref)):
        for r in range(rows):
            for t in range(INST):
                out_ref[r, :, t * cut : (t + 1) * cut] = jacobian_ref[t, r, k, :, :cut]
            left, right = (
                jacobian_ref[t, r, k, :, cut:].astype(jnp.float32) for t in range(INST)
            )
            out_ref[r, :, 2 * cut :] = tail_beside(held, left, right).astype(out_ref.dtype)


def here_kernel(tables_ref, adjoint_ref, near_ref, own_j_ref, near_j_ref, source_ref, out_ref):
    other = 1 - lax.rem(lax.axis_index("cell"), 2)
    for r in range(adjoint_ref.shape[0]):
        own = product(adjoint_ref[r], own_j_ref[r])
        block = chosen(tables_ref, NEAR_PICK + r, near_ref[other, 1], near_ref[other, 0])
        out_ref[r] = source_ref[r] - (own + product(block, near_j_ref[r]))


def update_kernel(
    last, tables_ref, far_ref, far_j_ref, peers_ref, partial_ref, adjoint_ref, volume_ref,
    step_ref, *outs
):
    rows = adjoint_ref.shape[0]
    copies = []
    for r in range(rows):
        block = chosen(tables_ref, FAR_PICK + r, far_ref[1], far_ref[0])
        flux = product(block, far_j_ref[r])
        same = cross = None
        for p in range(peers_ref.shape[0]):
            one = tables_ref[pl.ds(SAME + p, 1), :] * peers_ref[p, r]
            two = tables_ref[pl.ds(CROSS + p, 1), :] * peers_ref[p, r]
            same, cross = (one, two) if same is None else (same + one, cross + two)
        coupled = same + swapped(cross)
        scale = SCALE * volume_ref[pl.ds(r, 1), :]
        live = tables_ref[pl.ds(LIVE + r, 1), :]
        residual = live * (partial_ref[r] - flux - scale * coupled)
        new = adjoint_ref[r] + step_ref[pl.ds(r, 1), :] * residual
        if last:
            for value, out_ref in zip((new, residual), outs):
                out_ref[0, r] = left_of(value)
                out_ref[1, r] = left_of(swapped(value))
            continue
        outs[0][r] = new
        for p in range(peers_ref.shape[0]):
            outs[4][p, r] = new
        copies.append(send_copy(outs[4], outs[3], outs[5], r))
        copies[-1].start()
    if not last:
        for e in range(REACH):
            outs[1][e] = listed(tables_ref, NEAR_SEND, e, outs[0])
            outs[2][e] = listed(tables_ref, FAR_SEND, e, outs[0])
    for copy in copies:
        copy.wait()


def call(kernel, ins, outs, *args, scratch=()):
    spaces = {"s": SMEM, "v": VMEM, "a": HBM}
    return pl.pallas_call(
        kernel,
        in_specs=[spaces[c] for c in ins],
        out_specs=[spaces[c] for c, _ in outs],
        out_shape=[jax.ShapeDtypeStruct(*o) for _, o in outs],
        scratch_shapes=list(scratch),
        compiler_params=pltpu.CompilerParams(vmem_limit_bytes=4 << 20),
    )(*args)


def on_device(adjoint, source, jacobian, volume, step, slots, lists, pads):
    shape = adjoint.shape
    _, rows, objectives, width = shape
    peers = lax.axis_size("inst")
    cells = lax.axis_size("cell")
    near_groups = [[i, i + 1] for i in range(0, cells, 2)]
    far_pairs = [(i, (i + 1 if i % 2 else i - 1) % cells) for i in range(cells)]
    f32 = jnp.float32
    lanes = 2 * width
    block = ((rows, objectives, lanes), f32)
    halo = ((REACH, objectives, lanes), f32)
    gathered = ((peers,) + block[0], f32)
    sends = [pltpu.VMEM(*gathered), pltpu.SemaphoreType.DMA((rows,))]
    listed_out = (("v", block), ("v", halo), ("v", halo), ("a", gathered))
    held = pltpu.VMEM((objectives, TILE), f32)
    adjoint, near, far, spread = call(
        begin_kernel, "sv", listed_out, lists, adjoint, scratch=[held] + sends
    )
    cells_out = ("v", ((rows, lanes), f32))
    tables, source, volume, step = call(
        tables_kernel, "ssssvvv", (("v", ((TABLE, lanes), f32)), ("v", block)) + (cells_out,) * 2,
        slots, lists, pads, jnp.asarray(time_matrix()), source, volume, step, scratch=[held],
    )
    own_j, near_j, far_j = call(
        pack_kernel, "v", (("v", ((rows, width, lanes), jacobian.dtype)),) * 3, jacobian,
        scratch=[pltpu.VMEM((width, TILE), f32)],
    )
    for sweep in range(ITERS):
        last = sweep == ITERS - 1
        spread = lax.all_to_all(spread, "inst", 0, 0)
        far = lax.ppermute(far, "cell", far_pairs)
        near = lax.all_gather(near, "cell", axis_index_groups=near_groups)
        partial = call(
            here_kernel, "vvvvvv", (("v", block),), tables, adjoint, near, own_j, near_j, source
        )[0]
        result = call(
            functools.partial(update_kernel, last), "vvvvvvvv",
            (("v", (shape, f32)),) * 2 if last else listed_out,
            tables, far, far_j, spread, partial, adjoint, volume, step,
            scratch=[] if last else sends,
        )
        if last:
            return result[0], result[1]
        adjoint, near, far, spread = result


def solution(mesh):
    return jax.shard_map(
        on_device,
        mesh=mesh,
        in_specs=(
            P("inst", "cell", None, None),
            P("inst", "cell", None, None),
            P("inst", "cell", None, None, None),
            P("cell", None),
            P("cell", None),
            P("cell", None),
            P("cell"),
            P("cell"),
        ),
        out_specs=(P("inst", "cell", None, None), P("inst", "cell", None, None)),
        check_vma=False,
    )
```
